512 devices in a mesh: dp: 32 (over y, x), expert: 16 (over z, core).
Axes of the slice: x: 4, y: 8, z: 8, core: 2. Of those that a mesh axis runs over, the one named last changes fastest.
Arguments:
- grad_out: bfloat16 [4096, 3072], P(('dp', 'expert')), may hold values from -6 to 6
- routes: int32 [4096, 4], P(('dp', 'expert')), may hold values from 0 to 15, all different within a row; in each aligned block of 8 rows (0 to 7, 8 to 15, ...) at most 4 rows name the same one
- probs: bfloat16 [4096, 4], P(('dp', 'expert')), may hold values from 0.049804688 to 1
- hidden: bfloat16 [32, 16, 16, 4, 5376], P('dp', 'expert'), may hold values from -6 to 6
- w_down: bfloat16 [16, 5376, 3072], P('expert', 'dp'), may hold values from -0.078125 to 0.078125
Outputs:
- d_probs: float32 [4096, 4], P(('dp', 'expert'))
- d_hidden: bfloat16 [32, 16, 16, 4, 5376], P('dp', 'expert')
- d_down: float32 [16, 5376, 3072], P('expert', 'dp')
The draws below stay inside these ranges and needn't reach their ends.
Inputs may be any that keep to these rules, and one draw needn't show every extreme that they name: `routes`: each row names 4 different experts; among the rows of one device no expert is named more than 4 times, and exactly 4 times in some device.
All inputs are finite; a program needn't handle non-finite values.
Results may differ from the reference program's by a relative error of at most 0.0029.
Values may be sent and summed in bfloat16 or wider, within the bound.
No kernel may reach another device: no remote copies, remote signals or barrier semaphores. Data moves between devices by JAX's collectives and lax.ppermute only.
A program may use at most 64 MiB of HBM per device.

```python
import math
import jax
import jax.numpy as jnp
import numpy as np
from jax import lax

D = 3072
FFN = 5376
TOPK = 4
TOK_DEV = 8
EXPERTS = 16
CAP = 4
TOKENS = 4096
N_DP = 32
N_EXPERT = 16


def block_scale(own_key, dims, split, low, top_value):
    def one(dim, blocks):
        steps = jax.random.uniform(jax.random.fold_in(jax.random.fold_in(own_key, 6), dim), (blocks,), jnp.float32, low / len(split), top_value / len(split))
        return jnp.repeat(jnp.exp(steps), dims[dim] // blocks).reshape((-1,) + (1,) * (len(dims) - dim - 1))

    loudness = one(*split[0])
    for cut in split[1:]:
        loudness = loudness * one(*cut)
    return loudness


def shared_out(stream_key, own, number, rows, amount, top, reach, slope):
    sequence = jax.random.permutation(stream_key, amount)
    heavy_load, ordinary = load_shares(amount, rows * top, reach, slope, True), load_shares(amount, rows * top, reach, slope, False)
    places = jnp.arange(amount)

    def named(tallies, rotation):
        used = int((tallies > 0).sum())
        fixed = max(1, used // 4)
        passed = fixed + (places - fixed + rotation * (used - fixed)) % max(1, amount - fixed)
        return jnp.zeros((amount,), jnp.int32).at[sequence[jnp.where(places < fixed, places, passed)]].set(jnp.asarray(tallies, jnp.int32))

    tallies = jnp.where(number % 4 == 0, named(heavy_load, number // 4), named(ordinary, number - number // 4 - 1))
    mixed = jax.random.permutation(jax.random.fold_in(own, 3), amount)
    giver, receiver = mixed[0:amount // 2 * 2:2], mixed[1:amount // 2 * 2:2]
    margin = jnp.minimum(tallies[giver] - 1, reach - tallies[receiver]) // 2
    margin = jnp.where((giver == sequence[0]) | (receiver == sequence[0]) | (tallies[receiver] == 0), 0, jnp.maximum(margin, 0))
    passed = jax.random.randint(jax.random.fold_in(own, 4), (amount // 2,), 0, 1 << 20) % (margin + 1)
    tallies = tallies.at[giver].add(-passed).at[receiver].add(passed)
    members = jnp.searchsorted(jnp.cumsum(tallies), jnp.arange(rows * top), side="right").astype(jnp.int32)
    listing = members.reshape(top, rows).T
    listing = listing[jax.random.permutation(jax.random.fold_in(own, 1), rows)]
    rotation = jax.random.randint(jax.random.fold_in(own, 2), (rows, 1), 0, top)
    return jnp.take_along_axis(listing, (jnp.arange(top)[None, :] + rotation) % top, axis=1)


def load_shares(number_of, total, reach, slope, full):
    portions = [(1 << 20) // math.isqrt(rank ** slope) + 1 for rank in range(1, number_of + 1)]
    largest = reach if full else min(reach, max(-(-total // number_of), total * portions[0] // sum(portions)))
    least = 1 if total - largest >= number_of - 1 else 0
    counts, rest = [largest] + [least] * (number_of - 1), total - largest - least * (number_of - 1)
    while rest > 0:
        candidates = [i for i in range(1, number_of) if counts[i] < largest] or [i for i in range(1, number_of) if counts[i] < reach]
        whole, left = sum([portions[i] for i in candidates]), rest
        for i in candidates:
            addition = min(reach - counts[i], max(1, left * portions[i] // whole), rest)
            counts[i] = counts[i] + addition
            rest = rest - addition
    return np.array(counts)


def noise(key, dims, scale, limit, pieces=(), kind=jnp.bfloat16):
    gain = block_scale(key, dims, pieces, -0.22, 0.18) if pieces else 1.0
    entries = jax.random.normal(key, dims, jnp.float32) * scale * gain
    return jnp.minimum(jnp.maximum(entries, -limit), limit).astype(kind)


def setup_inputs(seed: int = 0) -> dict:
    key_of = jax.random.split(jax.random.key(seed), 6)
    grad_out = noise(key_of[0], (TOKENS, D), 1.0, 6.0, ((0, 512),))
    routes_keys = jax.random.split(jax.random.fold_in(key_of[1], 1), TOKENS // TOK_DEV)
    routes_turns = jax.random.permutation(jax.random.fold_in(key_of[1], 3), TOKENS // TOK_DEV)
    routes = jax.vmap(lambda own, number: shared_out(jax.random.fold_in(key_of[1], 2), own, number, TOK_DEV, EXPERTS, TOPK, CAP, 2))(routes_keys, routes_turns).reshape((TOKENS, TOPK))
    probs = jnp.clip(jnp.exp(math.log(1.0) - 2.9996462 * jax.random.uniform(key_of[2], (TOKENS, TOPK), jnp.float32) ** block_scale(key_of[2], (TOKENS, TOPK), ((0, 512),), -0.2, 0.2)), 0.049804688, 1.0).astype(jnp.bfloat16)
    hidden = noise(key_of[3], (N_DP, EXPERTS, N_EXPERT, CAP, FFN), 1.0, 6.0, ((0, 32), (1, 16)))
    w_down = noise(key_of[4], (EXPERTS, FFN, D), FFN ** -0.5, 0.078125, ((0, 16), (1, 32)))
    return dict(grad_out=grad_out, routes=routes, probs=probs, hidden=hidden, w_down=w_down)


def reference(grad_out, routes, probs, hidden, w_down):
    blocks = TOKENS // TOK_DEV
    flat = routes.reshape(blocks, TOK_DEV * TOPK)
    onehot = (flat[:, :, None] == jnp.arange(EXPERTS, dtype=jnp.int32)[None, None, :]).astype(jnp.int32)
    before = jnp.cumsum(onehot, axis=1) - onehot
    slot = jnp.sum(before * onehot, axis=2).astype(jnp.int32)
    block_id = jnp.arange(blocks, dtype=jnp.int32)[:, None]
    group = block_id // N_EXPERT
    source = block_id % N_EXPERT
    index = (((group * EXPERTS + flat) * N_EXPERT + source) * CAP + slot).reshape(-1).astype(jnp.int32)
    total = N_DP * EXPERTS * N_EXPERT * CAP
    token_of = (jnp.arange(TOKENS * TOPK, dtype=jnp.int32) // TOPK).astype(jnp.int32)
    token_at = jnp.zeros((total,), jnp.int32).at[index].set(token_of)
    live = jnp.zeros((total,), jnp.int32).at[index].set(1)
    dy_slot = jnp.where(live[:, None] > 0, grad_out[token_at], jnp.zeros((), jnp.bfloat16))
    p_slot = jnp.zeros((total,), jnp.float32).at[index].set(probs.reshape(-1).astype(jnp.float32))
    rows = N_EXPERT * CAP
    dy_slot = dy_slot.reshape(N_DP, EXPERTS, rows, D)
    p_slot = p_slot.reshape(N_DP, EXPERTS, rows)
    saved = hidden.reshape(N_DP, EXPERTS, rows, FFN)

    def per_expert(expert_id):
        dy_rows = dy_slot[:, expert_id].reshape(N_DP * rows, D)
        p_rows = p_slot[:, expert_id].reshape(N_DP * rows)
        h_rows = saved[:, expert_id].reshape(N_DP * rows, FFN)
        weight = w_down[expert_id]
        u = lax.dot_general(dy_rows, weight, (((1,), (1,)), ((), ())), preferred_element_type=jnp.float32)
        d_hid = (p_rows[:, None] * u).astype(jnp.bfloat16)
        part = jnp.sum(h_rows.astype(jnp.float32) * u, axis=1)
        g_rows = (p_rows[:, None] * dy_rows.astype(jnp.float32)).astype(jnp.bfloat16)
        d_weight = jnp.dot(h_rows.T, g_rows, preferred_element_type=jnp.float32)
        return d_hid, part, d_weight

    d_hid, part, d_down = lax.map(per_expert, jnp.arange(EXPERTS, dtype=jnp.int32))
    d_hidden = jnp.transpose(d_hid.reshape(EXPERTS, N_DP, N_EXPERT, CAP, FFN), (1, 0, 2, 3, 4))
    part_flat = jnp.transpose(part.reshape(EXPERTS, N_DP, rows), (1, 0, 2)).reshape(-1)
    d_probs = part_flat[index].reshape(TOKENS, TOPK)
    return d_probs, d_hidden, d_down
```

```python
import jax
import jax.numpy as jnp
from jax import lax
from jax.sharding import Mesh, PartitionSpec as P

YS, XS = 8, 4
F32, BF16 = jnp.float32, jnp.bfloat16


def shift(a, step):
    return lax.ppermute(a, "x", [(i, (i + step) % XS) for i in range(XS)])


def gather_w(w, x):
    n = w.shape[0]
    half = n // 16 * 8
    left, right = shift(w, 1), shift(w, -1)
    far_a, far_b = shift(left[:half], 1), shift(right[half:], -1)
    out = jnp.zeros((XS * n, w.shape[1]), w.dtype)
    put = lambda o, v, at: lax.dynamic_update_slice(o, v, (at, 0))
    out = put(out, w, x * n)
    out = put(out, left, (x + XS - 1) % XS * n)
    out = put(out, right, (x + 1) % XS * n)
    out = put(out, far_a, (x + 2) % XS * n)
    return put(out, far_b, (x + 2) % XS * n + half)


def body(grad_out, routes, probs, hidden, w_down):
    tok, width = grad_out.shape
    topk = routes.shape[1]
    cap, feat = hidden.shape[3], hidden.shape[4]
    nexp = lax.axis_size("expert")
    rows = nexp * cap
    share = w_down.shape[1]
    cols = XS * share
    x = lax.axis_index("x")

    w = w_down.reshape(share, width)
    w_cols = gather_w(w, x)

    flat = routes.reshape(-1)
    onehot = (flat[:, None] == jnp.arange(nexp, dtype=jnp.int32)[None, :]).astype(jnp.int32)
    before = jnp.cumsum(onehot, axis=0) - onehot
    slot = jnp.sum(before * onehot, axis=1)
    target = flat * cap + slot
    select = target[:, None] == jnp.arange(rows, dtype=jnp.int32)[None, :]
    sel_tok = jnp.sum(select.reshape(tok, topk, rows).astype(F32), axis=1).astype(BF16)
    dy_buf = jnp.dot(sel_tok.T, grad_out, preferred_element_type=F32).astype(BF16)
    p_buf = jnp.sum(jnp.where(select, probs.reshape(-1)[:, None].astype(F32), 0.0), axis=0)
    p_pad = jnp.broadcast_to(p_buf.astype(BF16)[:, None], (rows, 128))
    send = jnp.concatenate([dy_buf, p_pad], axis=1).reshape(nexp, cap, width + 128)
    recv = lax.all_to_all(send, "expert", split_axis=0, concat_axis=0, tiled=True)
    recv = recv.reshape(rows, width + 128)
    every = lax.all_gather(recv, "y", axis=0, tiled=True)

    h = hidden.reshape(rows, YS, cols).transpose(1, 0, 2)
    h, _ = lax.optimization_barrier((h, recv[:1, :1]))
    h = lax.all_to_all(h, "y", split_axis=0, concat_axis=0, tiled=True).reshape(YS * rows, cols)
    h_t = h.T

    dy = every[:, :width]
    p = every[:, width : width + 1].astype(F32)
    g = (p * dy.astype(F32)).astype(BF16)
    h_t, g = lax.optimization_barrier((h_t, g))

    def part(step):
        block = lax.dynamic_slice(h_t, ((x + step) % XS * share, 0), (share, YS * rows))
        return jnp.dot(block, g, preferred_element_type=F32)

    half = share // 16 * 8
    far = part(2).astype(BF16)
    from_a, from_b = shift(far[:half], 1), shift(far[half:], -1)
    up, down, own = part(1), part(3), part(0)
    up = jnp.concatenate([up[:half] + from_a.astype(F32), up[half:]], axis=0).astype(BF16)
    down = jnp.concatenate([down[:half], down[half:] + from_b.astype(F32)], axis=0).astype(BF16)
    d_down = own + shift(up, 1).astype(F32) + shift(down, -1).astype(F32)

    u = lax.dot_general(dy, w_cols, (((1,), (1,)), ((), ())), preferred_element_type=F32)
    dh = (p * u).astype(BF16)
    value = jnp.sum(h.astype(F32) * u, axis=1, keepdims=True)
    high = lax.reduce_precision(value, 8, 7)
    back = jnp.concatenate([dh, high.astype(BF16), (value - high).astype(BF16)], axis=1)
    back = lax.all_to_all(
        back.reshape(YS, rows, cols + 2), "y", split_axis=0, concat_axis=0, tiled=True
    )
    d_hidden = back[:, :, :cols].transpose(1, 0, 2).reshape(hidden.shape)
    d_slot = jnp.sum(back[:, :, cols:].astype(F32), axis=(0, 2))
    returned = lax.all_to_all(
        d_slot.reshape(nexp, cap), "expert", split_axis=0, concat_axis=0, tiled=True
    )
    d_probs = jnp.sum(jnp.where(select, returned.reshape(-1)[None, :], 0.0), axis=1)
    return d_probs.reshape(tok, topk), d_hidden, d_down.reshape(w_down.shape)


def solution(mesh):
    grid = Mesh(mesh.devices.reshape(YS, XS, -1), ("y", "x", "expert"))
    tokens = P(("y", "x", "expert"), None)
    saved = P(("y", "x"), "expert", None, None, None)
    weight = P("expert", ("y", "x"), None)
    return jax.shard_map(
        body,
        mesh=grid,
        in_specs=(tokens, tokens, tokens, saved, weight),
        out_specs=(tokens, saved, weight),
        check_vma=False,
    )
```

```python
import jax
import jax.numpy as jnp
from jax import lax
from jax.experimental import pallas as pl
from jax.experimental.pallas import tpu as pltpu
from jax.sharding import Mesh, PartitionSpec as P

YS, XS = 8, 4
F32, BF16 = jnp.float32, jnp.bfloat16
LANES = 128
TILE = 1536


def params(mib=60):
    return pltpu.CompilerParams(vmem_limit_bytes=mib * 1024 * 1024)


def shift(a, step):
    return lax.ppermute(a, "x", [(i, (i + step) % XS) for i in range(XS)])


def gather_w(w, x):
    n = w.shape[0]
    half = n // 32 * 16
    left, right = shift(w, 1), shift(w, -1)
    far_top, far_bottom = shift(left[:half], 1), shift(right[half:], -1)
    out = jnp.zeros((XS * n, w.shape[1]), w.dtype)
    put = lambda o, v, step, low: lax.dynamic_update_slice(o, v, ((x + step) % XS * n + low, 0))
    out = put(put(put(out, w, 0, 0), left, XS - 1, 0), right, 1, 0)
    return put(put(out, far_top, 2, 0), far_bottom, 2, half)


def pack(grad_out, routes, probs, me):
    tok, width = grad_out.shape
    topk = routes.shape[1]

    def kernel(me_ref, dy_ref, r_ref, p_ref, out_ref):
        out_ref[:, :width] = dy_ref[...]
        info = jnp.concatenate([r_ref[...].astype(F32), p_ref[...].astype(F32)], axis=0)
        info = jnp.concatenate([info] * (LANES // tok), axis=1)
        lane = lax.broadcasted_iota(jnp.int32, info.shape, 1)
        out_ref[:, width:] = jnp.where(lane // tok == me_ref[0], info, 0.0).astype(BF16)

    vmem = pl.BlockSpec(memory_space=pltpu.VMEM)
    return pl.pallas_call(
        kernel,
        out_shape=jax.ShapeDtypeStruct((tok, width + LANES), BF16),
        in_specs=[pl.BlockSpec(memory_space=pltpu.SMEM), vmem, vmem, vmem],
        out_specs=vmem,
        compiler_params=params(16),
        cost_estimate=pl.CostEstimate(flops=0, bytes_accessed=100000, transcendentals=0),
        name="pack_tokens",
    )(me, grad_out, routes.T, probs.T)


def pick_kernel(width, topk, tok, cap, me_ref, all_ref, _, out_ref):
    tokens = all_ref.shape[0]
    rows = out_ref.shape[0]
    me = me_ref[0].astype(F32)
    info = all_ref[:, width:].astype(F32)
    info = sum(info[at : at + tok] for at in range(0, tokens, tok))
    chosen = jnp.zeros((1, tokens), F32)
    weight = jnp.zeros((1, tokens), F32)
    for k in range(topk):
        hit = (info[k : k + 1] == me).astype(F32)
        chosen = chosen + hit
        weight = weight + hit * info[topk + k : topk + k + 1]
    older = lax.broadcasted_iota(jnp.int32, (tokens, tokens), 0)
    newer = lax.broadcasted_iota(jnp.int32, (tokens, tokens), 1)
    counts = ((older < newer) & (older // tok == newer // tok)).astype(BF16)
    many = jnp.broadcast_to(chosen, (16, tokens)).astype(BF16)
    before = jnp.dot(many, counts, preferred_element_type=F32)[:1]
    block = lax.broadcasted_iota(jnp.int32, (1, tokens), 1) // tok
    target = jnp.where(chosen > 0, block * cap + before.astype(jnp.int32), -1)
    select = lax.broadcasted_iota(jnp.int32, (rows, tokens), 0) == target
    p = jnp.sum(jnp.where(select, weight, 0.0), axis=1, keepdims=True)
    dy = jnp.dot(select.astype(F32).astype(BF16), all_ref[:, :width], preferred_element_type=F32)
    out_ref[:, :width] = dy.astype(BF16)
    out_ref[:, width:] = jnp.broadcast_to(p, (rows, LANES)).astype(BF16)


def pick(gathered, after, me, width, topk, tok, cap, rows):
    def kernel(*refs):
        pick_kernel(width, topk, tok, cap, *refs)

    return pl.pallas_call(
        kernel,
        out_shape=jax.ShapeDtypeStruct((rows, width + LANES), BF16),
        in_specs=[
            pl.BlockSpec(memory_space=pltpu.SMEM),
            pl.BlockSpec(memory_space=pltpu.VMEM),
            pl.BlockSpec(memory_space=pl.ANY),
        ],
        out_specs=pl.BlockSpec(memory_space=pltpu.VMEM),
        compiler_params=params(16),
        cost_estimate=pl.CostEstimate(
            flops=2 * rows * gathered.shape[0] * width, bytes_accessed=1300000, transcendentals=0
        ),
        name="pick_slots",
    )(me, gathered, after)


def down_parts(every, h_others, h_own, after, width):
    rows = every.shape[0]
    cols, share = h_others.shape[0], h_own.shape[0]

    def kernel(dy_ref, p_ref, others_ref, mine_ref, _, out_ref, own_ref):
        g = (p_ref[:, :1].astype(F32) * dy_ref[...].astype(F32)).astype(BF16)
        out_ref[...] = jnp.dot(others_ref[...], g, preferred_element_type=F32).astype(BF16)
        own_ref[...] = jnp.dot(mine_ref[...], g, preferred_element_type=F32)

    tile = lambda n: pl.BlockSpec((n, TILE), lambda i: (0, i))
    return pl.pallas_call(
        kernel,
        grid=(width // TILE,),
        out_shape=(
            jax.ShapeDtypeStruct((cols, width), BF16),
            jax.ShapeDtypeStruct((share, width), F32),
        ),
        in_specs=[
            tile(rows),
            pl.BlockSpec((rows, LANES), lambda i: (0, width // LANES)),
            pl.BlockSpec((cols, rows), lambda i: (0, 0)),
            pl.BlockSpec((share, rows), lambda i: (0, 0)),
            pl.BlockSpec(memory_space=pl.ANY),
        ],
        out_specs=(tile(cols), tile(share)),
        compiler_params=params(),
        cost_estimate=pl.CostEstimate(
            flops=2 * rows * cols * width, bytes_accessed=12000000, transcendentals=0
        ),
        name="down_parts",
    )(every, every, h_others, h_own, after)


def hidden_parts(every, w_cols, h, width, wide):
    rows = every.shape[0]
    cols = h.shape[1]
    steps = width // TILE
    edge = cols // LANES * LANES

    def kernel(dy_ref, p_ref, w_ref, h_ref, out_ref, acc):
        step = pl.program_id(0)
        term = lax.dot_general(
            dy_ref[...], w_ref[...], (((1,), (1,)), ((), ())), preferred_element_type=F32
        )

        @pl.when(step == 0)
        def _():
            acc[:, :cols] = term

        @pl.when(step > 0)
        def _():
            acc[:, :cols] += term

        @pl.when(step == steps - 1)
        def _():
            p = p_ref[:, :1].astype(F32)
            value = jnp.sum(h_ref[...].astype(F32) * acc[:, :cols], axis=1, keepdims=True)
            high = value.astype(BF16).astype(F32)
            lane = lax.broadcasted_iota(jnp.int32, (rows, wide - edge), 1) + edge
            tail = jnp.where(lane < cols, p * acc[:, edge:], 0.0)
            tail = jnp.where(lane == cols, high, jnp.where(lane == cols + 1, value - high, tail))
            out_ref[:, :edge] = (p * acc[:, :edge]).astype(BF16)
            out_ref[:, edge:] = tail.astype(BF16)

    return pl.pallas_call(
        kernel,
        grid=(steps,),
        out_shape=jax.ShapeDtypeStruct((rows, wide), BF16),
        in_specs=[
            pl.BlockSpec((rows, TILE), lambda i: (0, i)),
            pl.BlockSpec((rows, LANES), lambda i: (0, width // LANES)),
            pl.BlockSpec((cols, TILE), lambda i: (0, i)),
            pl.BlockSpec((rows, cols), lambda i: (0, 0)),
        ],
        out_specs=pl.BlockSpec((rows, wide), lambda i: (0, 0)),
        scratch_shapes=[pltpu.VMEM((rows, wide), F32)],
        compiler_params=params(),
        cost_estimate=pl.CostEstimate(
            flops=2 * rows * cols * width, bytes_accessed=9000000, transcendentals=0
        ),
        name="hidden_parts",
    )(every, every, w_cols, h)


def body(grad_out, routes, probs, hidden, w_down):
    tok, width = grad_out.shape
    topk = routes.shape[1]
    cap, feat = hidden.shape[3], hidden.shape[4]
    nexp = lax.axis_size("expert")
    rows = nexp * cap
    share = w_down.shape[1]
    cols = XS * share
    wide = -(-(cols + 2) // LANES) * LANES
    x = lax.axis_index("x")
    me = lax.axis_index("expert")

    h = hidden.reshape(nexp, cap, YS, cols).transpose(2, 0, 1, 3)
    h = lax.all_to_all(h, "y", split_axis=0, concat_axis=0, tiled=True)

    packed = lax.all_gather(pack(grad_out, routes, probs, me.reshape(1)), "expert", axis=0, tiled=True)
    mine = pick(packed, h, me.reshape(1), width, topk, tok, cap, rows)
    every = lax.all_gather(mine, "y", axis=0, tiled=True)

    w_cols = gather_w(w_down.reshape(share, width), x)
    h = h.reshape(YS * rows, cols)
    h_t = h.T
    h_own = lax.dynamic_slice(h_t, (x * share, 0), (share, YS * rows))
    h_others = lax.dynamic_update_slice(h_t, jnp.zeros_like(h_own), (x * share, 0))
    others, own = down_parts(every, h_others, h_own, w_cols, width)
    others = lax.psum_scatter(others, "x", scatter_dimension=0, tiled=True)
    d_down = own + others.astype(F32)

    back = hidden_parts(every, w_cols, h, width, wide)
    back = lax.all_to_all(
        back.reshape(YS, rows, wide), "y", split_axis=0, concat_axis=0, tiled=True
    )
    d_hidden = back[:, :, :cols].transpose(1, 0, 2).reshape(hidden.shape)
    d_slot = jnp.sum(back[:, :, cols : cols + 2].astype(F32), axis=(0, 2))
    returned = lax.all_to_all(
        d_slot.reshape(nexp, cap), "expert", split_axis=0, concat_axis=0, tiled=True
    )

    flat = routes.reshape(-1)
    onehot = (flat[:, None] == jnp.arange(nexp, dtype=jnp.int32)[None, :]).astype(jnp.int32)
    before = jnp.cumsum(onehot, axis=0) - onehot
    slot = jnp.sum(before * onehot, axis=1)
    select = (flat * cap + slot)[:, None] == jnp.arange(rows, dtype=jnp.int32)[None, :]
    d_probs = jnp.sum(jnp.where(select, returned.reshape(-1)[None, :], 0.0), axis=1)
    return d_probs.reshape(tok, topk), d_hidden, d_down.reshape(w_down.shape)


def solution(mesh):
    grid = Mesh(mesh.devices.reshape(YS, XS, -1), ("y", "x", "expert"))
    tokens = P(("y", "x", "expert"), None)
    saved = P(("y", "x"), "expert", None, None, None)
    weight = P("expert", ("y", "x"), None)
    return jax.shard_map(
        body,
        mesh=grid,
        in_specs=(tokens, tokens, tokens, saved, weight),
        out_specs=(tokens, saved, weight),
        check_vma=False,
    )
```

```python
import jax
import jax.numpy as jnp
from jax import lax
from jax.experimental import pallas as pl
from jax.experimental.pallas import tpu as pltpu
from jax.sharding import Mesh, PartitionSpec as P

YS, XS = 8, 4
F32, BF16 = jnp.float32, jnp.bfloat16
LANES = 128
TILE = 1536


def params(mib=52):
    return pltpu.CompilerParams(vmem_limit_bytes=mib * 1024 * 1024)


def shift(a, step):
    return lax.ppermute(a, "x", [(i, (i + step) % XS) for i in range(XS)])


def gather_w(w, x):
    n = w.shape[0]
    half = n // 32 * 16
    left, right = shift(w, 1), shift(w, -1)
    far_top, far_bottom = shift(left[:half], 1), shift(right[half:], -1)
    out = jnp.zeros((XS * n, w.shape[1]), w.dtype)
    put = lambda o, v, step, low: lax.dynamic_update_slice(o, v, ((x + step) % XS * n + low, 0))
    out = put(put(put(out, w, 0, 0), left, XS - 1, 0), right, 1, 0)
    return put(put(out, far_top, 2, 0), far_bottom, 2, half)


def pack(grad_out, routes, probs, me):
    tok, width = grad_out.shape
    topk = routes.shape[1]

    def kernel(me_ref, dy_ref, r_ref, p_ref, out_ref):
        out_ref[:, :width] = dy_ref[...]
        info = jnp.concatenate([r_ref[...].astype(F32), p_ref[...].astype(F32)], axis=0)
        info = jnp.concatenate([info] * (LANES // tok), axis=1)
        lane = lax.broadcasted_iota(jnp.int32, info.shape, 1)
        out_ref[:, width:] = jnp.where(lane // tok == me_ref[0], info, 0.0).astype(BF16)

    vmem = pl.BlockSpec(memory_space=pltpu.VMEM)
    return pl.pallas_call(
        kernel,
        out_shape=jax.ShapeDtypeStruct((tok, width + LANES), BF16),
        in_specs=[pl.BlockSpec(memory_space=pltpu.SMEM), vmem, vmem, vmem],
        out_specs=vmem,
        compiler_params=params(16),
        cost_estimate=pl.CostEstimate(flops=0, bytes_accessed=100000, transcendentals=0),
        name="pack_tokens",
    )(me, grad_out, routes.T, probs.T)


def pick_kernel(width, topk, tok, cap, me_ref, all_ref, _, out_ref):
    tokens = all_ref.shape[0]
    rows = out_ref.shape[0]
    me = me_ref[0].astype(F32)
    info = all_ref[:, width:].astype(F32)
    info = sum(info[at : at + tok] for at in range(0, tokens, tok))
    chosen = jnp.zeros((1, tokens), F32)
    weight = jnp.zeros((1, tokens), F32)
    for k in range(topk):
        hit = (info[k : k + 1] == me).astype(F32)
        chosen = chosen + hit
        weight = weight + hit * info[topk + k : topk + k + 1]
    older = lax.broadcasted_iota(jnp.int32, (tokens, tokens), 0)
    newer = lax.broadcasted_iota(jnp.int32, (tokens, tokens), 1)
    counts = ((older < newer) & (older // tok == newer // tok)).astype(BF16)
    many = jnp.broadcast_to(chosen, (16, tokens)).astype(BF16)
    before = jnp.dot(many, counts, preferred_element_type=F32)[:1]
    block = lax.broadcasted_iota(jnp.int32, (1, tokens), 1) // tok
    target = jnp.where(chosen > 0, block * cap + before.astype(jnp.int32), -1)
    select = lax.broadcasted_iota(jnp.int32, (rows, tokens), 0) == target
    p = jnp.sum(jnp.where(select, weight, 0.0), axis=1, keepdims=True)
    dy = jnp.dot(select.astype(F32).astype(BF16), all_ref[:, :width], preferred_element_type=F32)
    out_ref[:, :width] = dy.astype(BF16)
    out_ref[:, width:] = jnp.broadcast_to(p, (rows, LANES)).astype(BF16)


def pick(gathered, after, me, width, topk, tok, cap, rows):
    def kernel(*refs):
        pick_kernel(width, topk, tok, cap, *refs)

    return pl.pallas_call(
        kernel,
        out_shape=jax.ShapeDtypeStruct((rows, width + LANES), BF16),
        in_specs=[
            pl.BlockSpec(memory_space=pltpu.SMEM),
            pl.BlockSpec(memory_space=pltpu.VMEM),
            pl.BlockSpec(memory_space=pl.ANY),
        ],
        out_specs=pl.BlockSpec(memory_space=pltpu.VMEM),
        compiler_params=params(16),
        cost_estimate=pl.CostEstimate(
            flops=2 * rows * gathered.shape[0] * width, bytes_accessed=1300000, transcendentals=0
        ),
        name="pick_slots",
    )(me, gathered, after)


def down_parts(every, h_others, h_own, after, width):
    rows = every.shape[0]
    cols, share = h_others.shape[0], h_own.shape[0]

    def kernel(dy_ref, p_ref, others_ref, mine_ref, _, out_ref, own_ref):
        g = (p_ref[:, :1].astype(F32) * dy_ref[...].astype(F32)).astype(BF16)
        out_ref[...] = jnp.dot(others_ref[...], g, preferred_element_type=F32).astype(BF16)
        own_ref[...] = jnp.dot(mine_ref[...], g, preferred_element_type=F32)

    tile = lambda n: pl.BlockSpec((n, TILE), lambda i: (0, i))
    return pl.pallas_call(
        kernel,
        grid=(width // TILE,),
        out_shape=(
            jax.ShapeDtypeStruct((cols, width), BF16),
            jax.ShapeDtypeStruct((share, width), F32),
        ),
        in_specs=[
            tile(rows),
            pl.BlockSpec((rows, LANES), lambda i: (0, width // LANES)),
            pl.BlockSpec((cols, rows), lambda i: (0, 0)),
            pl.BlockSpec((share, rows), lambda i: (0, 0)),
            pl.BlockSpec(memory_space=pl.ANY),
        ],
        out_specs=(tile(cols), tile(share)),
        compiler_params=params(),
        cost_estimate=pl.CostEstimate(
            flops=2 * rows * cols * width, bytes_accessed=12000000, transcendentals=0
        ),
        name="down_parts",
    )(every, every, h_others, h_own, after)


def hidden_parts(every, w_cols, h, width, wide):
    rows = every.shape[0]
    cols = h.shape[1]
    steps = width // TILE
    edge = cols // LANES * LANES

    def kernel(dy_ref, p_ref, w_ref, h_ref, out_ref, acc):
        step = pl.program_id(0)
        term = lax.dot_general(
            dy_ref[...], w_ref[...], (((1,), (1,)), ((), ())), preferred_element_type=F32
        )

        @pl.when(step == 0)
        def _():
            acc[:, :cols] = term

        @pl.when(step > 0)
        def _():
            acc[:, :cols] += term

        @pl.when(step == steps - 1)
        def _():
            p = p_ref[:, :1].astype(F32)
            value = jnp.sum(h_ref[...].astype(F32) * acc[:, :cols], axis=1, keepdims=True)
            high = value.astype(BF16).astype(F32)
            lane = lax.broadcasted_iota(jnp.int32, (rows, wide - edge), 1) + edge
            tail = jnp.where(lane < cols, p * acc[:, edge:], 0.0)
            tail = jnp.where(lane == cols, high, jnp.where(lane == cols + 1, value - high, tail))
            out_ref[:, :edge] = (p * acc[:, :edge]).astype(BF16)
            out_ref[:, edge:] = tail.astype(BF16)

    return pl.pallas_call(
        kernel,
        grid=(steps,),
        out_shape=jax.ShapeDtypeStruct((rows, wide), BF16),
        in_specs=[
            pl.BlockSpec((rows, TILE), lambda i: (0, i)),
            pl.BlockSpec((rows, LANES), lambda i: (0, width // LANES)),
            pl.BlockSpec((cols, TILE), lambda i: (0, i)),
            pl.BlockSpec((rows, cols), lambda i: (0, 0)),
        ],
        out_specs=pl.BlockSpec((rows, wide), lambda i: (0, 0)),
        scratch_shapes=[pltpu.VMEM((rows, wide), F32)],
        compiler_params=params(),
        cost_estimate=pl.CostEstimate(
            flops=2 * rows * cols * width, bytes_accessed=9000000, transcendentals=0
        ),
        name="hidden_parts",
    )(every, every, w_cols, h)


def pick_probs(routes, values):
    tok, topk = routes.shape
    nexp, cap = values.shape

    def kernel(r_ref, v_ref, out_ref):
        fill = jnp.full((topk, LANES - tok), -1, jnp.int32)
        route = jnp.concatenate([r_ref[...], fill], axis=1)
        expert = lax.broadcasted_iota(jnp.int32, (nexp, LANES), 0)
        hits = [route[k : k + 1] == expert for k in range(topk)]
        chosen = sum(hit.astype(F32) for hit in hits)
        older = lax.broadcasted_iota(jnp.int32, (LANES, LANES), 0)
        newer = lax.broadcasted_iota(jnp.int32, (LANES, LANES), 1)
        slot = jnp.dot(
            chosen.astype(BF16), (older < newer).astype(BF16), preferred_element_type=F32
        )
        value = jnp.zeros((nexp, LANES), F32)
        for c in range(cap):
            value = jnp.where(slot == c, v_ref[:, c : c + 1], value)
        found = [jnp.sum(jnp.where(hit, value, 0.0), axis=0, keepdims=True) for hit in hits]
        out_ref[...] = jnp.concatenate(found, axis=0)[:, :tok]

    vmem = pl.BlockSpec(memory_space=pltpu.VMEM)
    return pl.pallas_call(
        kernel,
        out_shape=jax.ShapeDtypeStruct((topk, tok), F32),
        in_specs=[vmem, vmem],
        out_specs=vmem,
        compiler_params=params(16),
        cost_estimate=pl.CostEstimate(flops=0, bytes_accessed=20000, transcendentals=0),
        name="pick_probs",
    )(routes.T, values)


def body(grad_out, routes, probs, hidden, w_down):
    tok, width = grad_out.shape
    topk = routes.shape[1]
    cap, feat = hidden.shape[3], hidden.shape[4]
    nexp = lax.axis_size("expert")
    rows = nexp * cap
    share = w_down.shape[1]
    cols = XS * share
    wide = -(-(cols + 2) // LANES) * LANES
    x = lax.axis_index("x")
    me = lax.axis_index("expert")

    h = hidden.reshape(nexp, cap, YS, cols).transpose(2, 0, 1, 3)
    h = lax.all_to_all(h, "y", split_axis=0, concat_axis=0, tiled=True)

    packed = lax.all_gather(pack(grad_out, routes, probs, me.reshape(1)), "expert", axis=0, tiled=True)
    mine = pick(packed, h, me.reshape(1), width, topk, tok, cap, rows)
    every = lax.all_gather(mine, "y", axis=0, tiled=True)

    w_cols = gather_w(w_down.reshape(share, width), x)
    h = h.reshape(YS * rows, cols)
    h_t = h.T
    h_own = lax.dynamic_slice(h_t, (x * share, 0), (share, YS * rows))
    h_others = lax.dynamic_update_slice(h_t, jnp.zeros_like(h_own), (x * share, 0))
    others, own = down_parts(every, h_others, h_own, w_cols, width)
    others = lax.psum_scatter(others, "x", scatter_dimension=0, tiled=True)
    d_down = own + others.astype(F32)

    back = hidden_parts(every, w_cols, h, width, wide)
    back = lax.all_to_all(
        back.reshape(YS, rows, wide), "y", split_axis=0, concat_axis=0, tiled=True
    )
    d_hidden = back[:, :, :cols].transpose(1, 0, 2).reshape(hidden.shape)
    d_slot = jnp.sum(back[:, :, cols : cols + 2].astype(F32), axis=(0, 2))
    returned = lax.all_to_all(
        d_slot.reshape(nexp, cap), "expert", split_axis=0, concat_axis=0, tiled=True
    )

    d_probs = pick_probs(routes, returned.reshape(nexp, cap)).T
    return d_probs, d_hidden, d_down.reshape(w_down.shape)


def solution(mesh):
    grid = Mesh(mesh.devices.reshape(YS, XS, -1), ("y", "x", "expert"))
    tokens = P(("y", "x", "expert"), None)
    saved = P(("y", "x"), "expert", None, None, None)
    weight = P("expert", ("y", "x"), None)
    return jax.shard_map(
        body,
        mesh=grid,
        in_specs=(tokens, tokens, tokens, saved, weight),
        out_specs=(tokens, saved, weight),
        check_vma=False,
    )
```

```python
import jax
import jax.numpy as jnp
from jax import lax
from jax.experimental import pallas as pl
from jax.experimental.pallas import tpu as pltpu
from jax.sharding import Mesh, PartitionSpec as P

YS, XS = 8, 4
F32, BF16 = jnp.float32, jnp.bfloat16
LANES = 128
TILE = 1536


def params(mib=52):
    return pltpu.CompilerParams(vmem_limit_bytes=mib * 1024 * 1024)


def shift(a, step):
    return lax.ppermute(a, "x", [(i, (i + step) % XS) for i in range(XS)])


def gather_w(w, x):
    n = w.shape[0]
    half = n // 32 * 16
    left, right = shift(w, 1), shift(w, -1)
    far_top, far_bottom = shift(left[:half], 1), shift(right[half:], -1)
    out = jnp.zeros((XS * n, w.shape[1]), w.dtype)
    put = lambda o, v, step, low: lax.dynamic_update_slice(o, v, ((x + step) % XS * n + low, 0))
    out = put(put(put(out, w, 0, 0), left, XS - 1, 0), right, 1, 0)
    return put(put(out, far_top, 2, 0), far_bottom, 2, half)


def pack(grad_out, routes, probs, me):
    tok, width = grad_out.shape
    topk = routes.shape[1]

    def kernel(me_ref, dy_ref, r_ref, p_ref, out_ref):
        out_ref[:, :width] = dy_ref[...]
        info = jnp.concatenate([r_ref[...].astype(F32), p_ref[...].astype(F32)], axis=0)
        info = jnp.concatenate([info] * (LANES // tok), axis=1)
        lane = lax.broadcasted_iota(jnp.int32, info.shape, 1)
        out_ref[:, width:] = jnp.where(lane // tok == me_ref[0], info, 0.0).astype(BF16)

    vmem = pl.BlockSpec(memory_space=pltpu.VMEM)
    return pl.pallas_call(
        kernel,
        out_shape=jax.ShapeDtypeStruct((tok, width + LANES), BF16),
        in_specs=[pl.BlockSpec(memory_space=pltpu.SMEM), vmem, vmem, vmem],
        out_specs=vmem,
        compiler_params=params(16),
        cost_estimate=pl.CostEstimate(flops=0, bytes_accessed=100000, transcendentals=0),
        name="pack_tokens",
    )(me, grad_out, routes.T, probs.T)


def pick_kernel(width, topk, tok, cap, me_ref, all_ref, _, out_ref):
    tokens = all_ref.shape[0]
    rows = out_ref.shape[0]
    me = me_ref[0].astype(F32)
    info = all_ref[:, width:].astype(F32)
    info = sum(info[at : at + tok] for at in range(0, tokens, tok))
    chosen = jnp.zeros((1, tokens), F32)
    weight = jnp.zeros((1, tokens), F32)
    for k in range(topk):
        hit = (info[k : k + 1] == me).astype(F32)
        chosen = chosen + hit
        weight = weight + hit * info[topk + k : topk + k + 1]
    older = lax.broadcasted_iota(jnp.int32, (tokens, tokens), 0)
    newer = lax.broadcasted_iota(jnp.int32, (tokens, tokens), 1)
    counts = ((older < newer) & (older // tok == newer // tok)).astype(BF16)
    many = jnp.broadcast_to(chosen, (16, tokens)).astype(BF16)
    before = jnp.dot(many, counts, preferred_element_type=F32)[:1]
    block = lax.broadcasted_iota(jnp.int32, (1, tokens), 1) // tok
    target = jnp.where(chosen > 0, block * cap + before.astype(jnp.int32), -1)
    select = lax.broadcasted_iota(jnp.int32, (rows, tokens), 0) == target
    p = jnp.sum(jnp.where(select, weight, 0.0), axis=1, keepdims=True)
    dy = jnp.dot(select.astype(F32).astype(BF16), all_ref[:, :width], preferred_element_type=F32)
    out_ref[:, :width] = dy.astype(BF16)
    out_ref[:, width:] = jnp.broadcast_to(p, (rows, LANES)).astype(BF16)


def pick(gathered, after, me, width, topk, tok, cap, rows):
    def kernel(*refs):
        pick_kernel(width, topk, tok, cap, *refs)

    return pl.pallas_call(
        kernel,
        out_shape=jax.ShapeDtypeStruct((rows, width + LANES), BF16),
        in_specs=[
            pl.BlockSpec(memory_space=pltpu.SMEM),
            pl.BlockSpec(memory_space=pltpu.VMEM),
            pl.BlockSpec(memory_space=pl.ANY),
        ],
        out_specs=pl.BlockSpec(memory_space=pltpu.VMEM),
        compiler_params=params(16),
        cost_estimate=pl.CostEstimate(
            flops=2 * rows * gathered.shape[0] * width, bytes_accessed=1300000, transcendentals=0
        ),
        name="pick_slots",
    )(me, gathered, after)


def down_parts(every, h_others, after, width):
    rows = every.shape[0]
    cols = h_others.shape[0]

    def kernel(dy_ref, p_ref, others_ref, _, out_ref):
        g = (p_ref[:, :1].astype(F32) * dy_ref[...].astype(F32)).astype(BF16)
        out_ref[...] = jnp.dot(others_ref[...], g, preferred_element_type=F32).astype(BF16)

    tile = lambda n: pl.BlockSpec((n, TILE), lambda i: (0, i))
    return pl.pallas_call(
        kernel,
        grid=(width // TILE,),
        out_shape=jax.ShapeDtypeStruct((cols, width), BF16),
        in_specs=[
            tile(rows),
            pl.BlockSpec((rows, LANES), lambda i: (0, width // LANES)),
            pl.BlockSpec((cols, rows), lambda i: (0, 0)),
            pl.BlockSpec(memory_space=pl.ANY),
        ],
        out_specs=tile(cols),
        compiler_params=params(),
        cost_estimate=pl.CostEstimate(
            flops=2 * rows * cols * width, bytes_accessed=12000000, transcendentals=0
        ),
        name="down_parts",
    )(every, every, h_others, after)


def hidden_parts(every, w_cols, h, h_own, width, wide):
    rows = every.shape[0]
    cols, share = h.shape[1], h_own.shape[0]
    steps = width // TILE
    edge = cols // LANES * LANES

    def kernel(dy_ref, p_ref, w_ref, h_ref, mine_ref, out_ref, own_ref, acc):
        step = pl.program_id(0)
        g = (p_ref[:, :1].astype(F32) * dy_ref[...].astype(F32)).astype(BF16)
        own_ref[...] = jnp.dot(mine_ref[...], g, preferred_element_type=F32)
        term = lax.dot_general(
            dy_ref[...], w_ref[...], (((1,), (1,)), ((), ())), preferred_element_type=F32
        )

        @pl.when(step == 0)
        def _():
            acc[:, :cols] = term

        @pl.when(step > 0)
        def _():
            acc[:, :cols] += term

        @pl.when(step == steps - 1)
        def _():
            p = p_ref[:, :1].astype(F32)
            value = jnp.sum(h_ref[...].astype(F32) * acc[:, :cols], axis=1, keepdims=True)
            high = value.astype(BF16).astype(F32)
            lane = lax.broadcasted_iota(jnp.int32, (rows, wide - edge), 1) + edge
            tail = jnp.where(lane < cols, p * acc[:, edge:], 0.0)
            tail = jnp.where(lane == cols, high, jnp.where(lane == cols + 1, value - high, tail))
            out_ref[:, :edge] = (p * acc[:, :edge]).astype(BF16)
            out_ref[:, edge:] = tail.astype(BF16)

    return pl.pallas_call(
        kernel,
        grid=(steps,),
        out_shape=(
            jax.ShapeDtypeStruct((rows, wide), BF16),
            jax.ShapeDtypeStruct((share, width), F32),
        ),
        in_specs=[
            pl.BlockSpec((rows, TILE), lambda i: (0, i)),
            pl.BlockSpec((rows, LANES), lambda i: (0, width // LANES)),
            pl.BlockSpec((cols, TILE), lambda i: (0, i)),
            pl.BlockSpec((rows, cols), lambda i: (0, 0)),
            pl.BlockSpec((share, rows), lambda i: (0, 0)),
        ],
        out_specs=(
            pl.BlockSpec((rows, wide), lambda i: (0, 0)),
            pl.BlockSpec((share, TILE), lambda i: (0, i)),
        ),
        scratch_shapes=[pltpu.VMEM((rows, wide), F32)],
        compiler_params=params(),
        cost_estimate=pl.CostEstimate(
            flops=2 * rows * cols * width, bytes_accessed=9000000, transcendentals=0
        ),
        name="hidden_parts",
    )(every, every, w_cols, h, h_own)


def pick_probs(routes, values):
    tok, topk = routes.shape
    nexp, cap = values.shape

    def kernel(r_ref, v_ref, out_ref):
        fill = jnp.full((topk, LANES - tok), -1, jnp.int32)
        route = jnp.concatenate([r_ref[...], fill], axis=1)
        expert = lax.broadcasted_iota(jnp.int32, (nexp, LANES), 0)
        hits = [route[k : k + 1] == expert for k in range(topk)]
        chosen = sum(hit.astype(F32) for hit in hits)
        older = lax.broadcasted_iota(jnp.int32, (LANES, LANES), 0)
        newer = lax.broadcasted_iota(jnp.int32, (LANES, LANES), 1)
        slot = jnp.dot(
            chosen.astype(BF16), (older < newer).astype(BF16), preferred_element_type=F32
        )
        value = jnp.zeros((nexp, LANES), F32)
        for c in range(cap):
            value = jnp.where(slot == c, v_ref[:, c : c + 1], value)
        found = [jnp.sum(jnp.where(hit, value, 0.0), axis=0, keepdims=True) for hit in hits]
        out_ref[...] = jnp.concatenate(found, axis=0)[:, :tok]

    vmem = pl.BlockSpec(memory_space=pltpu.VMEM)
    return pl.pallas_call(
        kernel,
        out_shape=jax.ShapeDtypeStruct((topk, tok), F32),
        in_specs=[vmem, vmem],
        out_specs=vmem,
        compiler_params=params(16),
        cost_estimate=pl.CostEstimate(flops=0, bytes_accessed=20000, transcendentals=0),
        name="pick_probs",
    )(routes.T, values)


def body(grad_out, routes, probs, hidden, w_down):
    tok, width = grad_out.shape
    topk = routes.shape[1]
    cap, feat = hidden.shape[3], hidden.shape[4]
    nexp = lax.axis_size("expert")
    rows = nexp * cap
    share = w_down.shape[1]
    cols = XS * share
    wide = -(-(cols + 2) // LANES) * LANES
    x = lax.axis_index("x")
    me = lax.axis_index("expert")

    h = hidden.reshape(nexp, cap, YS, cols).transpose(2, 0, 1, 3)
    h = lax.all_to_all(h, "y", split_axis=0, concat_axis=0, tiled=True)

    packed = lax.all_gather(pack(grad_out, routes, probs, me.reshape(1)), "expert", axis=0, tiled=True)
    mine = pick(packed, h, me.reshape(1), width, topk, tok, cap, rows)
    every = lax.all_gather(mine, "y", axis=0, tiled=True)

    w_cols = gather_w(w_down.reshape(share, width), x)
    h = h.reshape(YS * rows, cols)
    h_t = h.T
    h_own = lax.dynamic_slice(h_t, (x * share, 0), (share, YS * rows))
    h_others = lax.dynamic_update_slice(h_t, jnp.zeros_like(h_own), (x * share, 0))
    others = down_parts(every, h_others, w_cols, width)
    others = lax.psum_scatter(others, "x", scatter_dimension=0, tiled=True)

    back, own = hidden_parts(every, w_cols, h, h_own, width, wide)
    back = lax.all_to_all(
        back.reshape(YS, rows, wide), "y", split_axis=0, concat_axis=0, tiled=True
    )
    d_hidden = back[:, :, :cols].transpose(1, 0, 2).reshape(hidden.shape)
    d_slot = jnp.sum(back[:, :, cols : cols + 2].astype(F32), axis=(0, 2))
    returned = lax.all_to_all(
        d_slot.reshape(nexp, cap), "expert", split_axis=0, concat_axis=0, tiled=True
    )

    d_probs = pick_probs(routes, returned.reshape(nexp, cap)).T
    d_down = own + others.astype(F32)
    return d_probs, d_hidden, d_down.reshape(w_down.shape)


def solution(mesh):
    grid = Mesh(mesh.devices.reshape(YS, XS, -1), ("y", "x", "expert"))
    tokens = P(("y", "x", "expert"), None)
    saved = P(("y", "x"), "expert", None, None, None)
    weight = P("expert", ("y", "x"), None)
    return jax.shard_map(
        body,
        mesh=grid,
        in_specs=(tokens, tokens, tokens, saved, weight),
        out_specs=(tokens, saved, weight),
        check_vma=False,
    )
```
